256 devices in a mesh: group: 8 (over z_lo, x), tp: 32 (over z_hi, y, core).
Axes of the slice: x: 4, y: 4, z: 8 (z_hi: 4, z_lo: 2; z = z_hi * 2 + z_lo), core: 2. Of those that a mesh axis runs over, the one named last changes fastest.
Arguments:
- tokens: bfloat16 [3584, 6144], P('group'), may hold values from -6 to 6
- routes: int32 [3584, 2], P('group'), may hold values from 0 to 7, as said below
- route_weights: float32 [3584, 2], P('group'), may hold values from 0.25 to 1
- ffn_weights: bfloat16 [1, 3, 6144, 8, 2048], P(None, None, 'tp', 'group'), may hold values from -0.078125 to 0.078125
Outputs:
- mixed: bfloat16 [3584, 6144], P(('group', 'tp'))
The draws below stay inside these ranges and needn't reach their ends.
Inputs may be any that keep to these rules, and one draw needn't show every extreme that they name: `routes`: each row names two different experts. Expert 0 is named by at most 392 of one group's 448 rows.
All inputs are finite; a program needn't handle non-finite values.
Results may differ from the reference program's by a relative error of at most 0.024.
Values may be sent and summed in bfloat16 or wider, within the bound.
A program may use at most 128 MiB of HBM per device.

```python
import jax
import jax.numpy as jnp
from jax import lax

D = 6144
EXPERTS = 8
EXP_WIN = 1
FO = 8
FI = 2048
TOK = 448
CAP = 392
TOKENS = 3584
N_TP = 32


def draw_routes(key, part):
    key = jax.random.fold_in(key, 11)
    keys = jax.random.split(key, 7)
    groups_count = TOKENS // TOK
    perms = jax.vmap(lambda subkey: jax.random.permutation(subkey, TOK))(jax.random.split(keys[0], groups_count))
    counts = CAP - jax.random.randint(keys[1], (groups_count, 2), 0, CAP // 2 + 1)
    chosen = jax.random.randint(keys[2], (), 0, groups_count * 2)
    flat_ids = jnp.arange(groups_count * 2, dtype=jnp.int32).reshape(groups_count, 2)
    counts = jnp.where(flat_ids == chosen, CAP, counts)
    shifts = jax.random.randint(keys[3], (groups_count, 2), 0, TOK)
    place_zero = (perms + shifts[:, 0:1]) % TOK < counts[:, 0:1]
    place_one = (perms + shifts[:, 1:2]) % TOK < counts[:, 1:2]
    other_one = jax.random.randint(keys[4], (groups_count, TOK), 2, EXPERTS)
    offset = jax.random.randint(keys[5], (groups_count, TOK), 1, EXPERTS - 2)
    other_two = 2 + (other_one - 2 + offset) % (EXPERTS - 2)
    col_first = jnp.where(place_zero, 0, jnp.where(place_one, 1, other_one))
    col_second = jnp.where(place_zero & place_one, 1, jnp.where(place_zero | place_one, other_one, other_two))
    swapped = jax.random.randint(keys[6], (groups_count, TOK), 0, 2) == 1
    first_col = jnp.where(swapped, col_second, col_first)
    second_col = jnp.where(swapped, col_first, col_second)
    return jnp.stack([first_col, second_col], -1).reshape(TOKENS, 2).astype(jnp.int32)


def level_of(own_key, dims, shards, least, high):
    def one(position, shards_of):
        heights = jax.random.uniform(jax.random.fold_in(jax.random.fold_in(own_key, 6), position), (shards_of,), jnp.float32, least / len(shards), high / len(shards))
        return jnp.repeat(jnp.exp(heights), dims[position] // shards_of).reshape((-1,) + (1,) * (len(dims) - position - 1))

    loudness = one(*shards[0])
    for cut in shards[1:]:
        loudness = loudness * one(*cut)
    return loudness


def bell_draw(rng, shape, spread, limit, cuts=(), kind=jnp.bfloat16):
    result = jax.random.normal(rng, shape, jnp.float32) * spread
    if len(cuts) > 0:
        result = level_of(rng, shape, cuts, -0.22, 0.18) * result
    return jnp.clip(result, min=-limit, max=limit).astype(kind)


def setup_inputs(seed: int = 0) -> dict:
    key_list = jax.random.split(jax.random.key(seed), 5)
    tokens = bell_draw(key_list[0], (TOKENS, D), 1.0, 6.0, ((0, 8),))
    routes = draw_routes(jax.random.fold_in(key_list[4], 71), 0)
    route_weights = jnp.clip(0.25 + 0.75 * jax.random.uniform(key_list[2], (TOKENS, 2), jnp.float32) ** level_of(key_list[2], (TOKENS, 2), ((0, 8),), -0.2, 0.2), 0.25, 1.0)
    ffn_weights = bell_draw(key_list[3], (EXP_WIN, 3, D, FO, FI), D ** -0.5, 0.078125, ((2, 32), (3, 8)))
    return {"tokens": tokens, "routes": routes, "route_weights": route_weights, "ffn_weights": ffn_weights}


def reference(tokens, routes, route_weights, ffn_weights):
    slice_cols = FI // N_TP
    mix_rows = []
    for expert in range(EXP_WIN):
        mix_rows.append(jnp.sum(jnp.where(routes == expert, route_weights, 0.0), axis=1))
    mix_table = jnp.stack(mix_rows)

    def slice_term(summed, slice_id):
        partial_value = jnp.zeros((tokens.shape[0], D), jnp.float32)
        for expert in range(EXP_WIN):
            weight_block = lax.dynamic_slice_in_dim(ffn_weights[expert], slice_id * slice_cols, slice_cols, 3)
            weight_block = weight_block.reshape(3, D, FO * slice_cols)
            gate_out = jnp.dot(tokens, weight_block[0], preferred_element_type=jnp.float32)
            up_out = jnp.dot(tokens, weight_block[1], preferred_element_type=jnp.float32)
            hidden = (jax.nn.silu(gate_out) * up_out).astype(jnp.bfloat16)
            projected = lax.dot_general(hidden, weight_block[2], (((1,), (1,)), ((), ())), preferred_element_type=jnp.float32)
            partial_value = partial_value + mix_table[expert][:, None] * projected
        rounded = lax.optimization_barrier(partial_value.astype(jnp.bfloat16))
        return summed + rounded.astype(jnp.float32), None

    summed, _ = lax.scan(slice_term, jnp.zeros((tokens.shape[0], D), jnp.float32), jnp.arange(N_TP, dtype=jnp.int32))
    return summed.astype(jnp.bfloat16)
```

```python
import jax
import jax.numpy as jnp
from jax import lax
from jax.experimental import pallas as pl
from jax.experimental.pallas import tpu as pltpu
from jax.sharding import PartitionSpec as P

MESH = pl.DeviceIdType.MESH
NX, NY, NZ, NC = 4, 4, 8, 2
OWN = 14
PAD = 16


def dev(x, y, z, c):
    x, y, z = lax.rem(x + 2 * NX, NX), lax.rem(y + 2 * NY, NY), lax.rem(z + 2 * NZ, NZ)
    return ((z % 2) * NX + x, ((z // 2) * NY + y) * NC + c)


def take(ref, sem):
    pltpu.make_async_copy(ref, ref, sem).wait()


def kernel(tok_hbm, w_hbm, out_ref, tok, gu, wd, px, pr, po, hid, acc, st, rv, fin, fo,
           tok_sem, tk_ss, tk_rs, a_ss, a_rs, xo_ss, x_rs, xf_ss, w_ss, w_rs, wo_ss, wx_rs, wf_ss,
           p_ss, p_rs, h_ss, h_rs, s_ss, s_rs, r_ss, r_rs, f_ss, f_rs):
    grp, tp = lax.axis_index("group"), lax.axis_index("tp")
    z_lo, x = grp // NX, grp % NX
    c, y, z_hi = tp % NC, (tp // NC) % NY, tp // (NC * NY)
    z = z_hi * 2 + z_lo
    rows = tok.shape[1]
    half = tok.shape[2]
    piece = w_hbm.shape[1]
    hrows = rows // 2
    dcols = acc.shape[2]

    def send(src, dst, ss, rs, to):
        pltpu.make_async_remote_copy(
            src_ref=src, dst_ref=dst, send_sem=ss, recv_sem=rs, device_id=to, device_id_type=MESH
        ).start()

    right, left = dev(x + 1, y, z, c), dev(x - 1, y, z, c)
    up, down = dev(x, y, z + 1, c), dev(x, y, z - 1, c)
    sib = dev(x, y, z, 1 - c)
    mycols = pl.ds(pl.multiple_of(c * half, 128), half)
    load = pltpu.make_async_copy(tok_hbm.at[:, mycols], tok.at[z_lo], tok_sem)
    load.start()

    bar = pltpu.get_barrier_semaphore()
    me = (z * NY + y) * NC + c
    plane = NZ * NY * NC

    def hello(i, _):
        j = lax.rem(me + i, plane)
        to = dev(x, (j // NC) % NY, j // (NC * NY), j % NC)
        pl.semaphore_signal(bar, inc=1, device_id=to, device_id_type=MESH)
        return 0

    lax.fori_loop(1, plane, hello, 0)
    pl.semaphore_signal(bar, inc=1, device_id=right, device_id_type=MESH)
    pl.semaphore_signal(bar, inc=1, device_id=left, device_id_type=MESH)
    pl.semaphore_wait(bar, plane + 1)

    src_slot = (z_hi % 2) * 8 + y * NC + c
    src_rows = pl.ds(pl.multiple_of(src_slot * piece, 64), piece)

    def a_send(n, _):
        q = n // NY
        dz = (1 + 2 * (q // 2)) * (1 - 2 * (q % 2))
        tz, ty = lax.rem(z + dz + NZ, NZ), lax.rem(y + n % NY, NY)
        lanes = pl.ds(pl.multiple_of((ty * 4 + tz // 2) * 128, 128), 128)
        send(w_hbm.at[pl.ds(0, 2), :, lanes], gu.at[0, :, src_rows, :], a_ss, a_rs.at[src_slot],
             dev(x, ty, tz, z_hi // 2))
        return 0

    lax.fori_loop(0, 16, a_send, 0)

    wz, wc = 2 * z_hi + y // 2, y % 2
    w_dst = wd.at[0, pl.ds(pl.multiple_of(c * piece, 64), piece),
                  pl.ds(pl.multiple_of(z_lo * 512, 128), 512)]
    for j in range(NY):
        ty = lax.rem(y + j, NY)
        src = w_hbm.at[2, :, pl.ds(pl.multiple_of(ty * 512, 128), 512)]
        rs = w_rs.at[z_lo * NC + c]
        if j == 0:
            here = jnp.logical_and(wz == z, wc == c)

            @pl.when(here)
            def _():
                pltpu.make_async_copy(src, w_dst, rs).start()

            @pl.when(jnp.logical_not(here))
            def _():
                send(src, w_dst, w_ss.at[0], rs, dev(x, ty, wz, wc))
        else:
            send(src, w_dst, w_ss.at[j], rs, dev(x, ty, wz, wc))

    for k, to in ((0, up), (1, down)):
        r = pl.ds(k * hrows, hrows)
        send(tok_hbm.at[r, mycols], tok.at[z_lo, r], tk_ss.at[k], tk_rs.at[k], to)

    same = 1 - (z_hi // 2 + c) % 2
    m0 = (z_hi + 1 + same) % 2

    def slot_of(n):
        return ((m0 + n // 4) % 2) * 8 + lax.rem(y - n % 4 + NY, NY) * NC

    def pc(k, s):
        return gu.at[k, :, pl.ds(pl.multiple_of(s * piece, 64), piece), :]

    def x_own(n):
        for core in range(NC):
            s = slot_of(n) + core
            take(pc(0, s), a_rs.at[s])
            send(pc(0, s), pc(1, s), xo_ss.at[0], x_rs.at[0, s], right)
            send(pc(0, s), pc(2, s), xo_ss.at[1], x_rs.at[1, s], left)

    def x_fwd(n):
        s = slot_of(n)
        take(pc(1, s), x_rs.at[0, s])
        send(pc(1, s), pc(3, s), xf_ss.at[0], x_rs.at[2, s], right)
        take(pc(2, s + 1), x_rs.at[1, s + 1])
        send(pc(2, s + 1), pc(3, s + 1), xf_ss.at[1], x_rs.at[2, s + 1], left)

    lag = 2
    for n in range(lag):
        x_own(n)

    def x_loop(n, _):
        x_own(n)
        x_fwd(n - lag)
        return 0

    lax.fori_loop(lag, 8, x_loop, 0)

    def wpc(k, i):
        return wd.at[k, pl.ds((i % NC) * piece, piece), pl.ds((i // NC) * 512, 512)]

    for i in range(4):
        take(wpc(0, i), w_rs.at[i])
        send(wpc(0, i), wpc(1, i), wo_ss.at[0], wx_rs.at[0, i], right)
        send(wpc(0, i), wpc(2, i), wo_ss.at[1], wx_rs.at[1, i], left)
    for n in range(8 - lag, 8):
        x_fwd(n)

    load.wait()
    for k in range(2):
        r = pl.ds(k * hrows, hrows)
        take(tok.at[1 - z_lo, r], tk_rs.at[k])

    lane = pl.ds(pl.multiple_of(((1 - z_lo) * 4 + z_hi) * 128, 128), 128)

    def gate_up(r):
        if r == 1:
            for n in range(8):
                take(pc(1, 2 * n + 1), x_rs.at[0, 2 * n + 1])
        if r == 2:
            for n in range(8):
                take(pc(2, 2 * n), x_rs.at[1, 2 * n])
        if r == 3:
            for n in range(16):
                take(pc(3, n), x_rs.at[2, n])
        rhs = jnp.concatenate([gu[r, 0], gu[r, 1]], axis=1)
        px[r] = jnp.dot(tok[1 - c], rhs, preferred_element_type=jnp.float32)
        send(px.at[r], pr.at[r], p_ss.at[r], p_rs.at[r], sib)
        po[...] = jnp.dot(tok[c], rhs, preferred_element_type=jnp.float32)
        take(pr.at[r], p_rs.at[r])
        gate = po[:, :128] + pr[r, :, :128]
        upv = po[:, 128:] + pr[r, :, 128:]
        hid[c, r, :, lane] = (gate / (1.0 + jnp.exp(-gate)) * upv).astype(jnp.bfloat16)
        own = hid.at[c, r, :, lane]
        send(own, own, h_ss.at[r, 0, 0], h_rs.at[r, 0, 1], up)
        send(own, own, h_ss.at[r, 1, 0], h_rs.at[r, 1, 1], down)
        send(own, own, s_ss.at[r], s_rs.at[r], sib)

    def ring(r, d):
        for k, to in ((0, up), (1, down)):
            zs = lax.rem(z + (d if k else NZ - d), NZ)
            ln = pl.ds(pl.multiple_of(((1 - zs % 2) * 4 + zs // 2) * 128, 128), 128)
            part = pl.ds(k * hrows, hrows)
            got = hid.at[c, r, part, ln] if d == 4 else hid.at[c, r, :, ln]
            take(got, h_rs.at[r, k, d])
            if d < 3:
                send(got, got, h_ss.at[r, k, d], h_rs.at[r, k, d + 1], to)
            elif d == 3:
                more = hid.at[c, r, part, ln]
                send(more, more, h_ss.at[r, k, d], h_rs.at[r, k, d + 1], to)
            send(got, got, s_ss.at[r], s_rs.at[r], sib)

    def wd_fwd():
        for i in range(0, 4, 2):
            take(wpc(1, i), wx_rs.at[0, i])
            send(wpc(1, i), wpc(3, i), wf_ss.at[0], wx_rs.at[2, i], right)
            take(wpc(2, i + 1), wx_rs.at[1, i + 1])
            send(wpc(2, i + 1), wpc(3, i + 1), wf_ss.at[1], wx_rs.at[2, i + 1], left)

    def project(r):
        take(hid.at[1 - c, r], s_rs.at[r])
        if r == 1:
            for i in (1, 3):
                take(wpc(1, i), wx_rs.at[0, i])
        if r == 2:
            for i in (0, 2):
                take(wpc(2, i), wx_rs.at[1, i])
        if r == 3:
            for i in range(4):
                take(wpc(3, i), wx_rs.at[2, i])
        for g in range(2):
            term = lax.dot_general(hid[g, r], wd[r], (((1,), (1,)), ((), ())),
                                   preferred_element_type=jnp.float32)
            if r == 0:
                acc[g, pl.ds(0, rows)] = term
            else:
                acc[g, pl.ds(0, rows)] += term

    gate_up(0)
    gate_up(1)
    ring(0, 1)
    gate_up(2)
    ring(0, 2)
    ring(1, 1)
    gate_up(3)
    ring(0, 3)
    ring(1, 2)
    ring(2, 1)
    wd_fwd()
    ring(0, 4)
    ring(1, 3)
    ring(2, 2)
    ring(3, 1)
    project(0)
    ring(1, 4)
    ring(2, 3)
    ring(3, 2)
    project(1)
    ring(2, 4)
    ring(3, 3)
    project(2)
    ring(3, 4)
    project(3)

    acc[:, pl.ds(rows, 8)] = jnp.zeros((2, 8, dcols), jnp.float32)
    for ty in range(NY):
        for k in range(16):
            g, th, tc = k // 8, (k % 8) // 2, k % 2
            first = ((th * NY + ty) * NC + tc) * OWN
            st[ty, pl.ds(k * PAD, PAD)] = acc[g, pl.ds(first, PAD)].astype(jnp.bfloat16)
    for d in range(1, NY):
        ty = lax.rem(y + d, NY)
        send(st.at[ty], rv.at[3 - d], r_ss.at[d - 1], r_rs.at[3 - d], dev(x, ty, z, c))
    for k in range(3):
        take(rv.at[k], r_rs.at[k])
    total = st[y].astype(jnp.float32)
    for k in range(3):
        total += rv[k].astype(jnp.float32)
    fin[...] = total.astype(jnp.bfloat16)

    cols = pl.ds(pl.multiple_of((z * NC + c) * dcols, 128), dcols)

    def place(k, _):
        tz, tc = 2 * ((k % 8) // 2) + k // 8, k % 2
        src = fin.at[pl.ds(pl.multiple_of(k * PAD, PAD), PAD)]
        here = jnp.logical_and(tz == z, tc == c)

        @pl.when(here)
        def _():
            pltpu.make_async_copy(src, fo.at[:, cols], f_rs).start()

        @pl.when(jnp.logical_not(here))
        def _():
            send(src, fo.at[:, cols], f_ss, f_rs, dev(x, y, tz, tc))

        return 0

    lax.fori_loop(0, 16, place, 0)
    take(fo, f_rs)
    out_ref[...] = fo[...]

    take(w_hbm.at[pl.ds(0, 2)], a_ss)
    for j in range(NY):
        src = w_hbm.at[2, :, pl.ds(0, 512)]
        if j == 0:
            @pl.when(jnp.logical_not(jnp.logical_and(wz == z, wc == c)))
            def _():
                take(src, w_ss.at[0])
        else:
            take(src, w_ss.at[j])
    for k in range(2):
        take(tok.at[0, pl.ds(0, hrows)], tk_ss.at[k])
        take(gu.at[0], xo_ss.at[k])
        take(gu.at[0, 0], xf_ss.at[k])
        take(wd.at[0], wo_ss.at[k])
        take(wd.at[0, pl.ds(0, piece)], wf_ss.at[k])
    for r in range(4):
        take(px.at[r], p_ss.at[r])
        take(hid.at[c, r], s_ss.at[r])
        for k in range(2):
            for d in range(4):
                h = hrows if d == 3 else rows
                take(hid.at[c, r, pl.ds(0, h), lane], h_ss.at[r, k, d])
    for k in range(3):
        take(rv.at[k], r_ss.at[k])
    take(fin.at[pl.ds(0, 15 * PAD)], f_ss)


def per_device(tokens, routes, route_weights, ffn_weights):
    rows, width = tokens.shape
    w = ffn_weights.reshape(ffn_weights.shape[1], ffn_weights.shape[2], ffn_weights.shape[4])
    piece = w.shape[1]
    half = width // 2
    dcols = width // 16
    bf, f32 = jnp.bfloat16, jnp.float32
    dma = pltpu.SemaphoreType.DMA
    summed = pl.pallas_call(
        kernel,
        out_shape=jax.ShapeDtypeStruct((PAD, width), bf),
        in_specs=[pl.BlockSpec(memory_space=pl.ANY)] * 2,
        out_specs=pl.BlockSpec(memory_space=pltpu.VMEM),
        scratch_shapes=[
            pltpu.VMEM((2, rows, half), bf),
            pltpu.VMEM((4, 2, half, 128), bf),
            pltpu.VMEM((4, 2 * piece, 1024), bf),
            pltpu.VMEM((4, rows, 256), f32),
            pltpu.VMEM((4, rows, 256), f32),
            pltpu.VMEM((rows, 256), f32),
            pltpu.VMEM((2, 4, rows, 1024), bf),
            pltpu.VMEM((2, rows + 8, dcols), f32),
            pltpu.VMEM((NY, 16 * PAD, dcols), bf),
            pltpu.VMEM((3, 16 * PAD, dcols), bf),
            pltpu.VMEM((16 * PAD, dcols), bf),
            pltpu.VMEM((PAD, width), bf),
            dma,
            dma((2,)),
            dma((2,)),
            dma,
            dma((16,)),
            dma((2,)),
            dma((3, 16)),
            dma((2,)),
            dma((4,)),
            dma((4,)),
            dma((2,)),
            dma((3, 4)),
            dma((2,)),
            dma((4,)),
            dma((4,)),
            dma((4, 2, 4)),
            dma((4, 2, 5)),
            dma((4,)),
            dma((4,)),
            dma((3,)),
            dma((3,)),
            dma,
            dma,
        ],
        compiler_params=pltpu.CompilerParams(
            collective_id=0, has_side_effects=True, vmem_limit_bytes=56 * 2**20
        ),
    )(tokens, w)
    first = lax.axis_index("tp") * OWN
    matched = lax.dynamic_slice_in_dim(routes, first, OWN) == 0
    weights = lax.dynamic_slice_in_dim(route_weights, first, OWN)
    mix = jnp.sum(jnp.where(matched, weights, 0.0), axis=1)
    return (summed[:OWN].astype(f32) * mix[:, None]).astype(bf)


def solution(mesh):
    placed = (
        P("group", None),
        P("group", None),
        P("group", None),
        P(None, None, "tp", "group", None),
    )
    return jax.shard_map(
        per_device, mesh=mesh, in_specs=placed, out_specs=P(("group", "tp"), None), check_vma=False
    )
```

```python
import jax
import jax.numpy as jnp
from jax import lax
from jax.experimental import pallas as pl
from jax.experimental.pallas import tpu as pltpu
from jax.sharding import PartitionSpec as P

MESH = pl.DeviceIdType.MESH
NX, NY, NZ, NC = 4, 4, 8, 2
OWN = 14
PAD = 16


def dev(x, y, z, c):
    x, y, z = lax.rem(x + 2 * NX, NX), lax.rem(y + 2 * NY, NY), lax.rem(z + 2 * NZ, NZ)
    return ((z % 2) * NX + x, ((z // 2) * NY + y) * NC + c)


def take(ref, sem):
    pltpu.make_async_copy(ref, ref, sem).wait()


def kernel(tok_hbm, w_hbm, out_ref, tok, gu, wd, px, pr, po, hid, acc, st, rv, fin, fo,
           tok_sem, tk_ss, tk_rs, a_ss, a_rs, xo_ss, x_rs, xf_ss, w_ss, w_rs, wo_ss, wx_rs, wf_ss,
           p_ss, p_rs, h_ss, h_rs, s_ss, s_rs, r_ss, r_rs, f_ss, f_rs, ty_ss, ty_rs):
    grp, tp = lax.axis_index("group"), lax.axis_index("tp")
    z_lo, x = grp // NX, grp % NX
    c, y, z_hi = tp % NC, (tp // NC) % NY, tp // (NC * NY)
    z = z_hi * 2 + z_lo
    rows = tok.shape[1]
    half = tok.shape[2]
    piece = w_hbm.shape[1]
    hrows = rows // 2
    dcols = acc.shape[2]

    def send(src, dst, ss, rs, to):
        pltpu.make_async_remote_copy(
            src_ref=src, dst_ref=dst, send_sem=ss, recv_sem=rs, device_id=to, device_id_type=MESH
        ).start()

    right, left = dev(x + 1, y, z, c), dev(x - 1, y, z, c)
    up, down = dev(x, y, z + 1, c), dev(x, y, z - 1, c)
    sib = dev(x, y, z, 1 - c)
    chunk = half // 4

    def at_hbm(k):
        return pl.ds(pl.multiple_of((2 * k + c) * chunk, 128), chunk)

    for k in range(4):
        pltpu.make_async_copy(
            tok_hbm.at[:, at_hbm(k)], tok.at[z_lo, :, pl.ds(k * chunk, chunk)], tok_sem
        ).start()

    bar = pltpu.get_barrier_semaphore()
    me = (z * NY + y) * NC + c
    plane = NZ * NY * NC

    def hello(i, _):
        j = lax.rem(me + i, plane)
        to = dev(x, (j // NC) % NY, j // (NC * NY), j % NC)
        pl.semaphore_signal(bar, inc=1, device_id=to, device_id_type=MESH)
        return 0

    lax.fori_loop(1, plane, hello, 0)
    pl.semaphore_signal(bar, inc=1, device_id=right, device_id_type=MESH)
    pl.semaphore_signal(bar, inc=1, device_id=left, device_id_type=MESH)
    pl.semaphore_wait(bar, plane + 1)

    src_slot = z_hi * 4 + (y % 2) * NC + c
    src_rows = pl.ds(pl.multiple_of(src_slot * piece, 64), piece)

    def a_wave(w):
        far = 1 + 2 * (w // 2)
        for dy in (w % 2, w % 2 + 2):
            for dz in (far, -far):
                ty, tz = lax.rem(y + dy, NY), lax.rem(z + dz + NZ, NZ)
                lanes = pl.ds(pl.multiple_of((ty * 4 + tz // 2) * 128, 128), 128)
                send(w_hbm.at[pl.ds(0, 2), :, lanes], gu.at[0, :, src_rows, :], a_ss,
                     a_rs.at[src_slot], dev(x, ty, tz, y // 2))

    wz, wc = 2 * z_hi + c, y // 2
    w_here = jnp.logical_and(wz == z, wc == c)
    w_dst = wd.at[0, pl.ds(pl.multiple_of((y % 2) * piece, 64), piece),
                  pl.ds(pl.multiple_of(z_lo * 512, 128), 512)]

    def w_send():
        for j in range(NY):
            ty = lax.rem(y + j, NY)
            src = w_hbm.at[2, :, pl.ds(pl.multiple_of(ty * 512, 128), 512)]
            rs = w_rs.at[z_lo * 2 + y % 2]
            if j == 0:
                @pl.when(w_here)
                def _():
                    pltpu.make_async_copy(src, w_dst, rs).start()

                @pl.when(jnp.logical_not(w_here))
                def _():
                    send(src, w_dst, w_ss.at[0], rs, dev(x, ty, wz, wc))
            else:
                send(src, w_dst, w_ss.at[j], rs, dev(x, ty, wz, wc))

    quarter = rows // NY

    def quarter_of(yy):
        return pl.ds(pl.multiple_of(yy * quarter, PAD), quarter)

    def tok_send():
        for k in range(4):
            send(tok_hbm.at[quarter_of(y), at_hbm(k)],
                 tok.at[z_lo, quarter_of(y), pl.ds(k * chunk, chunk)],
                 tk_ss.at[k // 2], tk_rs.at[k // 2], down if k // 2 else up)

    def tok_pass():
        for k in range(2):
            take(tok.at[1 - z_lo, quarter_of(y), pl.ds(2 * k * chunk, 2 * chunk)], tk_rs.at[k])
        for d in range(1, NY):
            mine = tok.at[1 - z_lo, quarter_of(y)]
            send(mine, mine, ty_ss.at[d - 1], ty_rs.at[d - 1], dev(x, y + d, z, c))

    def tok_wait():
        take(tok.at[z_lo], tok_sem)
        for d in range(1, NY):
            take(tok.at[1 - z_lo, quarter_of(lax.rem(y - d + NY, NY))], ty_rs.at[d - 1])

    def slot_of(w, m):
        far = (1 + 2 * (w // 2)) * (1 - 2 * m)
        return (lax.rem(z - far + NZ, NZ) // 2) * 4 + ((y + w) % 2) * NC

    def pc(k, s):
        return gu.at[k, :, pl.ds(pl.multiple_of(s * piece, 64), piece), :]

    def x_own(w):
        for m in range(2):
            for core in range(NC):
                s = slot_of(w, m) + core
                take(pc(0, s), a_rs.at[s])
                send(pc(0, s), pc(1, s), xo_ss.at[0], x_rs.at[0, s], right)
                send(pc(0, s), pc(2, s), xo_ss.at[1], x_rs.at[1, s], left)

    def x_fwd(w):
        for m in range(2):
            s = slot_of(w, m)
            take(pc(1, s), x_rs.at[0, s])
            send(pc(1, s), pc(3, s), xf_ss.at[0], x_rs.at[2, s], right)
            take(pc(2, s + 1), x_rs.at[1, s + 1])
            send(pc(2, s + 1), pc(3, s + 1), xf_ss.at[1], x_rs.at[2, s + 1], left)

    def wpc(k, i):
        return wd.at[k, pl.ds(pl.multiple_of((i % 2) * piece, 64), piece),
                     pl.ds(pl.multiple_of((i // 2) * 512, 128), 512)]

    near = z_lo * 2
    far = 2 - near

    def w_own(first):
        for i in (first, first + 1):
            take(wpc(0, i), w_rs.at[i])
            send(wpc(0, i), wpc(1, i), wo_ss.at[0], wx_rs.at[0, i], right)
            send(wpc(0, i), wpc(2, i), wo_ss.at[1], wx_rs.at[1, i], left)

    def w_fwd(i):
        take(wpc(1, i), wx_rs.at[0, i])
        send(wpc(1, i), wpc(3, i), wf_ss.at[0], wx_rs.at[2, i], right)
        take(wpc(2, i + 1), wx_rs.at[1, i + 1])
        send(wpc(2, i + 1), wpc(3, i + 1), wf_ss.at[1], wx_rs.at[2, i + 1], left)

    lane = pl.ds(pl.multiple_of(((1 - z_lo) * 4 + z_hi) * 128, 128), 128)

    def gate_up(r):
        if r == 1:
            for n in range(8):
                take(pc(1, 2 * n + 1), x_rs.at[0, 2 * n + 1])
        if r == 2:
            for n in range(8):
                take(pc(2, 2 * n), x_rs.at[1, 2 * n])
        if r == 3:
            for n in range(16):
                take(pc(3, n), x_rs.at[2, n])
        rhs = jnp.concatenate([gu[r, 0], gu[r, 1]], axis=1)
        px[r] = jnp.dot(tok[1 - c], rhs, preferred_element_type=jnp.float32)
        send(px.at[r], pr.at[r], p_ss.at[r], p_rs.at[r], sib)
        po[...] = jnp.dot(tok[c], rhs, preferred_element_type=jnp.float32)
        take(pr.at[r], p_rs.at[r])
        gate = po[:, :128] + pr[r, :, :128]
        upv = po[:, 128:] + pr[r, :, 128:]
        hid[c, r, :, lane] = (gate / (1.0 + jnp.exp(-gate)) * upv).astype(jnp.bfloat16)
        own = hid.at[c, r, :, lane]
        send(own, own, h_ss.at[r, 0, 0], h_rs.at[r, 0, 1], up)
        send(own, own, h_ss.at[r, 1, 0], h_rs.at[r, 1, 1], down)
        send(own, own, s_ss.at[r], s_rs.at[r], sib)

    def ring(r, d):
        for k, to in ((0, up), (1, down)):
            zs = lax.rem(z + (d if k else NZ - d), NZ)
            ln = pl.ds(pl.multiple_of(((1 - zs % 2) * 4 + zs // 2) * 128, 128), 128)
            part = pl.ds(k * hrows, hrows)
            got = hid.at[c, r, part, ln] if d == 4 else hid.at[c, r, :, ln]
            take(got, h_rs.at[r, k, d])
            if d < 3:
                send(got, got, h_ss.at[r, k, d], h_rs.at[r, k, d + 1], to)
            elif d == 3:
                more = hid.at[c, r, part, ln]
                send(more, more, h_ss.at[r, k, d], h_rs.at[r, k, d + 1], to)
            send(got, got, s_ss.at[r], s_rs.at[r], sib)

    def ready(r):
        take(hid.at[1 - c, r], s_rs.at[r])
        if r == 1:
            for i in (1, 3):
                take(wpc(1, i), wx_rs.at[0, i])
        if r == 2:
            for i in (0, 2):
                take(wpc(2, i), wx_rs.at[1, i])
        if r == 3:
            for i in range(4):
                take(wpc(3, i), wx_rs.at[2, i])

    def project(r, g):
        term = lax.dot_general(hid[g, r], wd[r], (((1,), (1,)), ((), ())),
                               preferred_element_type=jnp.float32)
        if r == 0:
            acc[g, pl.ds(0, rows)] = term
        else:
            acc[g, pl.ds(0, rows)] += term

    acc[:, pl.ds(rows, 8)] = jnp.zeros((2, 8, dcols), jnp.float32)
    a_wave(0)
    pl.when(c == z_lo)(w_send)
    x_own(0)
    tok_send()
    w_own(near)
    tok_pass()
    a_wave(1)
    a_wave(2)
    pl.when(c != z_lo)(w_send)
    x_own(1)
    a_wave(3)
    x_fwd(0)
    x_fwd(1)
    w_fwd(near)
    x_own(2)
    x_fwd(2)
    x_own(3)
    tok_wait()
    gate_up(0)
    ring(0, 1)
    x_fwd(3)
    w_own(far)
    ring(0, 2)
    gate_up(1)
    gate_up(2)
    ring(0, 3)
    gate_up(3)
    ring(1, 1)
    ring(2, 1)
    ring(3, 1)
    ring(0, 4)
    ring(1, 2)
    ring(2, 2)
    ring(3, 2)
    w_fwd(far)
    ring(1, 3)
    ring(2, 3)
    ring(3, 3)
    ready(0)
    project(0, 0)
    project(0, 1)
    ring(1, 4)
    ring(2, 4)
    ready(1)
    project(1, 0)
    project(1, 1)
    ring(3, 4)
    ready(2)
    project(2, 0)
    project(2, 1)
    ready(3)

    for g in range(2):
        project(3, g)
        for ty in range(NY):
            for k in range(8):
                first = (((k // 2) * NY + ty) * NC + k % 2) * OWN
                st[g, ty, pl.ds(k * PAD, PAD)] = acc[g, pl.ds(first, PAD)].astype(jnp.bfloat16)
        for d in range(1, NY):
            ty = lax.rem(y + d, NY)
            send(st.at[g, ty], rv.at[g, 3 - d], r_ss.at[g, d - 1], r_rs.at[g, 3 - d], dev(x, ty, z, c))

    cols = pl.ds(pl.multiple_of((z * NC + c) * dcols, 128), dcols)
    for g in range(2):
        total = st[g, y].astype(jnp.float32)
        for k in range(3):
            take(rv.at[g, k], r_rs.at[g, k])
            total += rv[g, k].astype(jnp.float32)
        fin[g] = total.astype(jnp.bfloat16)

        def place(k, _):
            tz, tc = 2 * (k // 2) + g, k % 2
            src = fin.at[g, pl.ds(pl.multiple_of(k * PAD, PAD), PAD)]
            here = jnp.logical_and(tz == z, tc == c)

            @pl.when(here)
            def _():
                pltpu.make_async_copy(src, fo.at[:, cols], f_rs).start()

            @pl.when(jnp.logical_not(here))
            def _():
                send(src, fo.at[:, cols], f_ss, f_rs, dev(x, y, tz, tc))

            return 0

        lax.fori_loop(0, 8, place, 0)
    take(fo, f_rs)
    for n in range(2 * NZ * NC):
        zh, yy, core = n // 8, (n // 2) % 4, n % 2
        at = (((2 * zh + core) * NC + yy // 2) * 2 + yy % 2) * piece
        out_ref[:, n * piece:(n + 1) * piece] = fo[:, at:at + piece]

    take(w_hbm.at[pl.ds(0, 2)], a_ss)
    for j in range(NY):
        src = w_hbm.at[2, :, pl.ds(0, 512)]
        if j == 0:
            @pl.when(jnp.logical_not(w_here))
            def _():
                take(src, w_ss.at[0])
        else:
            take(src, w_ss.at[j])
    for k in range(2):
        take(tok.at[0, pl.ds(0, quarter), pl.ds(0, 2 * chunk)], tk_ss.at[k])
        take(gu.at[0], xo_ss.at[k])
        take(gu.at[0, 0], xf_ss.at[k])
        take(wd.at[0], wo_ss.at[k])
        take(wd.at[0, pl.ds(0, piece)], wf_ss.at[k])
    for r in range(4):
        take(px.at[r], p_ss.at[r])
        take(hid.at[c, r], s_ss.at[r])
        for k in range(2):
            for d in range(4):
                h = hrows if d == 3 else rows
                take(hid.at[c, r, pl.ds(0, h), lane], h_ss.at[r, k, d])
    for k in range(3):
        take(tok.at[0, pl.ds(0, quarter)], ty_ss.at[k])
        for g in range(2):
            take(rv.at[g, k], r_ss.at[g, k])
    take(fin.at[0], f_ss)
    take(fin.at[1, pl.ds(0, 7 * PAD)], f_ss)


def per_device(tokens, routes, route_weights, ffn_weights):
    rows, width = tokens.shape
    w = ffn_weights.reshape(ffn_weights.shape[1], ffn_weights.shape[2], ffn_weights.shape[4])
    piece = w.shape[1]
    half = width // 2
    dcols = width // 16
    bf, f32 = jnp.bfloat16, jnp.float32
    dma = pltpu.SemaphoreType.DMA
    summed = pl.pallas_call(
        kernel,
        out_shape=jax.ShapeDtypeStruct((PAD, width), bf),
        in_specs=[pl.BlockSpec(memory_space=pl.ANY)] * 2,
        out_specs=pl.BlockSpec(memory_space=pltpu.VMEM),
        scratch_shapes=[
            pltpu.VMEM((2, rows, half), bf),
            pltpu.VMEM((4, 2, half, 128), bf),
            pltpu.VMEM((4, 2 * piece, 1024), bf),
            pltpu.VMEM((4, rows, 256), f32),
            pltpu.VMEM((4, rows, 256), f32),
            pltpu.VMEM((rows, 256), f32),
            pltpu.VMEM((2, 4, rows, 1024), bf),
            pltpu.VMEM((2, rows + 8, dcols), f32),
            pltpu.VMEM((2, NY, 8 * PAD, dcols), bf),
            pltpu.VMEM((2, 3, 8 * PAD, dcols), bf),
            pltpu.VMEM((2, 8 * PAD, dcols), bf),
            pltpu.VMEM((PAD, width), bf),
            dma,
            dma((2,)),
            dma((2,)),
            dma,
            dma((16,)),
            dma((2,)),
            dma((3, 16)),
            dma((2,)),
            dma((4,)),
            dma((4,)),
            dma((2,)),
            dma((3, 4)),
            dma((2,)),
            dma((4,)),
            dma((4,)),
            dma((4, 2, 4)),
            dma((4, 2, 5)),
            dma((4,)),
            dma((4,)),
            dma((2, 3)),
            dma((2, 3)),
            dma,
            dma,
            dma((3,)),
            dma((3,)),
        ],
        compiler_params=pltpu.CompilerParams(
            collective_id=0, has_side_effects=True, vmem_limit_bytes=56 * 2**20
        ),
    )(tokens, w)
    first = lax.axis_index("tp") * OWN
    matched = lax.dynamic_slice_in_dim(routes, first, OWN) == 0
    weights = lax.dynamic_slice_in_dim(route_weights, first, OWN)
    mix = jnp.sum(jnp.where(matched, weights, 0.0), axis=1)
    return (summed[:OWN].astype(f32) * mix[:, None]).astype(bf)


def solution(mesh):
    placed = (
        P("group", None),
        P("group", None),
        P("group", None),
        P(None, None, "tp", "group", None),
    )
    return jax.shard_map(
        per_device, mesh=mesh, in_specs=placed, out_specs=P(("group", "tp"), None), check_vma=False
    )
```

```python
import jax
import jax.numpy as jnp
from jax import lax
from jax.experimental import pallas as pl
from jax.experimental.pallas import tpu as pltpu
from jax.sharding import PartitionSpec as P

MESH = pl.DeviceIdType.MESH
NX, NY, NZ, NC = 4, 4, 8, 2
OWN = 14
PAD = 16


def dev(x, y, z, c):
    x, y, z = lax.rem(x + 2 * NX, NX), lax.rem(y + 2 * NY, NY), lax.rem(z + 2 * NZ, NZ)
    return ((z % 2) * NX + x, ((z // 2) * NY + y) * NC + c)


def take(ref, sem):
    pltpu.make_async_copy(ref, ref, sem).wait()


def kernel(tok_hbm, w_hbm, out_ref, tok, gu, wd, px, pr, po, hid, acc, st, rv, fin, fo,
           tok_sem, tk_ss, tk_rs, a_ss, a_rs, xo_ss, x_rs, xf_ss, w_ss, w_rs, wo_ss, wx_rs, wf_ss,
           p_ss, p_rs, h_ss, h_rs, s_ss, s_rs, r_ss, r_rs, f_ss, f_rs, ty_ss, ty_rs):
    grp, tp = lax.axis_index("group"), lax.axis_index("tp")
    z_lo, x = grp // NX, grp % NX
    c, y, z_hi = tp % NC, (tp // NC) % NY, tp // (NC * NY)
    z = z_hi * 2 + z_lo
    rows = tok.shape[1]
    half = tok.shape[2]
    piece = w_hbm.shape[1]
    hrows = rows // 2
    dcols = acc.shape[2]

    def send(src, dst, ss, rs, to):
        pltpu.make_async_remote_copy(
            src_ref=src, dst_ref=dst, send_sem=ss, recv_sem=rs, device_id=to, device_id_type=MESH
        ).start()

    right, left = dev(x + 1, y, z, c), dev(x - 1, y, z, c)
    up, down = dev(x, y, z + 1, c), dev(x, y, z - 1, c)
    north, south = dev(x, y + 1, z, c), dev(x, y - 1, z, c)
    sib = dev(x, y, z, 1 - c)
    chunk = half // 4

    def at_hbm(k):
        return pl.ds(pl.multiple_of((2 * k + c) * chunk, 128), chunk)

    for k in range(4):
        pltpu.make_async_copy(
            tok_hbm.at[:, at_hbm(k)], tok.at[z_lo, :, pl.ds(k * chunk, chunk)], tok_sem
        ).start()

    bar = pltpu.get_barrier_semaphore()
    me = (z * NY + y) * NC + c
    plane = NZ * NY * NC

    def hello(i, _):
        j = lax.rem(me + i, plane)
        to = dev(x, (j // NC) % NY, j // (NC * NY), j % NC)
        pl.semaphore_signal(bar, inc=1, device_id=to, device_id_type=MESH)
        return 0

    lax.fori_loop(1, plane, hello, 0)
    pl.semaphore_signal(bar, inc=1, device_id=right, device_id_type=MESH)
    pl.semaphore_signal(bar, inc=1, device_id=left, device_id_type=MESH)
    pl.semaphore_wait(bar, plane + 1)

    src_slot = z_hi * 4 + (y % 2) * NC + c
    src_rows = pl.ds(pl.multiple_of(src_slot * piece, 64), piece)

    def a_wave(w):
        far = 1 + 2 * (w // 2)
        for dy in (w % 2, w % 2 + 2):
            for dz in (far, -far):
                ty, tz = lax.rem(y + dy, NY), lax.rem(z + dz + NZ, NZ)
                lanes = pl.ds(pl.multiple_of((ty * 4 + tz // 2) * 128, 128), 128)
                send(w_hbm.at[pl.ds(0, 2), :, lanes], gu.at[0, :, src_rows, :], a_ss,
                     a_rs.at[src_slot], dev(x, ty, tz, y // 2))

    wz, wc = 2 * z_hi + c, y // 2
    w_here = jnp.logical_and(wz == z, wc == c)
    w_dst = wd.at[0, pl.ds(pl.multiple_of((y % 2) * piece, 64), piece),
                  pl.ds(pl.multiple_of(z_lo * 512, 128), 512)]

    def w_send():
        for j in range(NY):
            ty = lax.rem(y + j, NY)
            src = w_hbm.at[2, :, pl.ds(pl.multiple_of(ty * 512, 128), 512)]
            rs = w_rs.at[z_lo * 2 + y % 2]
            if j == 0:
                @pl.when(w_here)
                def _():
                    pltpu.make_async_copy(src, w_dst, rs).start()

                @pl.when(jnp.logical_not(w_here))
                def _():
                    send(src, w_dst, w_ss.at[0], rs, dev(x, ty, wz, wc))
            else:
                send(src, w_dst, w_ss.at[j], rs, dev(x, ty, wz, wc))

    quarter = rows // NY

    def quarter_of(yy):
        return pl.ds(pl.multiple_of(yy * quarter, PAD), quarter)

    def tok_send():
        for k in range(4):
            send(tok_hbm.at[quarter_of(y), at_hbm(k)],
                 tok.at[z_lo, quarter_of(y), pl.ds(k * chunk, chunk)],
                 tk_ss.at[k // 2], tk_rs.at[k // 2], down if k // 2 else up)

    def tok_pass():
        for k in range(2):
            take(tok.at[1 - z_lo, quarter_of(y), pl.ds(2 * k * chunk, 2 * chunk)], tk_rs.at[k])
        mine = tok.at[1 - z_lo, quarter_of(y)]
        send(mine, mine, ty_ss.at[0], ty_rs.at[0], north)
        send(mine, mine, ty_ss.at[1], ty_rs.at[1], south)

    def tok_fwd():
        for k, to in ((0, north), (1, south)):
            yy = quarter_of(lax.rem(y + (1 if k else NY - 1), NY))
            take(tok.at[1 - z_lo, yy], ty_rs.at[k])
            part = tok.at[1 - z_lo, yy, pl.ds(2 * k * chunk, 2 * chunk)]
            send(part, part, ty_ss.at[2 + k], ty_rs.at[2 + k], to)

    def tok_wait():
        take(tok.at[z_lo], tok_sem)
        for k in range(2):
            yy = quarter_of(lax.rem(y + 2, NY))
            take(tok.at[1 - z_lo, yy, pl.ds(2 * k * chunk, 2 * chunk)], ty_rs.at[2 + k])

    def slot_of(w, m):
        far = (1 + 2 * (w // 2)) * (1 - 2 * m)
        return (lax.rem(z - far + NZ, NZ) // 2) * 4 + ((y + w) % 2) * NC

    def pc(k, s):
        return gu.at[k, :, pl.ds(pl.multiple_of(s * piece, 64), piece), :]

    def x_own(w):
        for m in range(2):
            for core in range(NC):
                s = slot_of(w, m) + core
                take(pc(0, s), a_rs.at[s])
                send(pc(0, s), pc(1, s), xo_ss.at[0], x_rs.at[0, s], right)
                send(pc(0, s), pc(2, s), xo_ss.at[1], x_rs.at[1, s], left)

    def x_fwd(w):
        for m in range(2):
            s = slot_of(w, m)
            take(pc(1, s), x_rs.at[0, s])
            send(pc(1, s), pc(3, s), xf_ss.at[0], x_rs.at[2, s], right)
            take(pc(2, s + 1), x_rs.at[1, s + 1])
            send(pc(2, s + 1), pc(3, s + 1), xf_ss.at[1], x_rs.at[2, s + 1], left)

    def wpc(k, i):
        return wd.at[k, pl.ds(pl.multiple_of((i % 2) * piece, 64), piece),
                     pl.ds(pl.multiple_of((i // 2) * 512, 128), 512)]

    near = z_lo * 2
    far = 2 - near

    def w_own(first):
        for i in (first, first + 1):
            take(wpc(0, i), w_rs.at[i])
            send(wpc(0, i), wpc(1, i), wo_ss.at[0], wx_rs.at[0, i], right)
            send(wpc(0, i), wpc(2, i), wo_ss.at[1], wx_rs.at[1, i], left)

    def w_fwd(i):
        take(wpc(1, i), wx_rs.at[0, i])
        send(wpc(1, i), wpc(3, i), wf_ss.at[0], wx_rs.at[2, i], right)
        take(wpc(2, i + 1), wx_rs.at[1, i + 1])
        send(wpc(2, i + 1), wpc(3, i + 1), wf_ss.at[1], wx_rs.at[2, i + 1], left)

    lane = pl.ds(pl.multiple_of(((1 - z_lo) * 4 + z_hi) * 128, 128), 128)

    def gate_up(r):
        if r == 1:
            for n in range(8):
                take(pc(1, 2 * n + 1), x_rs.at[0, 2 * n + 1])
        if r == 2:
            for n in range(8):
                take(pc(2, 2 * n), x_rs.at[1, 2 * n])
        if r == 3:
            for n in range(16):
                take(pc(3, n), x_rs.at[2, n])
        rhs = jnp.concatenate([gu[r, 0], gu[r, 1]], axis=1)
        px[r] = jnp.dot(tok[1 - c], rhs, preferred_element_type=jnp.float32)
        send(px.at[r], pr.at[r], p_ss.at[r], p_rs.at[r], sib)
        po[...] = jnp.dot(tok[c], rhs, preferred_element_type=jnp.float32)
        take(pr.at[r], p_rs.at[r])
        gate = po[:, :128] + pr[r, :, :128]
        upv = po[:, 128:] + pr[r, :, 128:]
        hid[c, r, :, lane] = (gate / (1.0 + jnp.exp(-gate)) * upv).astype(jnp.bfloat16)
        own = hid.at[c, r, :, lane]
        send(own, own, h_ss.at[r, 0, 0], h_rs.at[r, 0, 1], up)
        send(own, own, h_ss.at[r, 1, 0], h_rs.at[r, 1, 1], down)
        send(own, own, s_ss.at[r], s_rs.at[r], sib)

    def ring(r, d):
        for k, to in ((0, up), (1, down)):
            zs = lax.rem(z + (d if k else NZ - d), NZ)
            ln = pl.ds(pl.multiple_of(((1 - zs % 2) * 4 + zs // 2) * 128, 128), 128)
            part = pl.ds(k * hrows, hrows)
            got = hid.at[c, r, part, ln] if d == 4 else hid.at[c, r, :, ln]
            take(got, h_rs.at[r, k, d])
            if d < 3:
                send(got, got, h_ss.at[r, k, d], h_rs.at[r, k, d + 1], to)
            elif d == 3:
                more = hid.at[c, r, part, ln]
                send(more, more, h_ss.at[r, k, d], h_rs.at[r, k, d + 1], to)
            send(got, got, s_ss.at[r], s_rs.at[r], sib)

    def ready(r):
        take(hid.at[1 - c, r], s_rs.at[r])
        if r == 1:
            for i in (1, 3):
                take(wpc(1, i), wx_rs.at[0, i])
        if r == 2:
            for i in (0, 2):
                take(wpc(2, i), wx_rs.at[1, i])
        if r == 3:
            for i in range(4):
                take(wpc(3, i), wx_rs.at[2, i])

    def project(r, g):
        term = lax.dot_general(hid[g, r], wd[r], (((1,), (1,)), ((), ())),
                               preferred_element_type=jnp.float32)
        if r == 0:
            acc[g, pl.ds(0, rows)] = term
        else:
            acc[g, pl.ds(0, rows)] += term

    acc[:, pl.ds(rows, 8)] = jnp.zeros((2, 8, dcols), jnp.float32)
    a_wave(0)
    pl.when(c == z_lo)(w_send)
    x_own(0)
    tok_send()
    a_wave(1)
    tok_pass()
    a_wave(2)
    x_fwd(0)
    x_own(1)
    x_fwd(1)
    a_wave(3)
    tok_fwd()
    x_own(2)
    pl.when(c != z_lo)(w_send)
    x_fwd(2)
    x_own(3)
    tok_wait()
    gate_up(0)
    x_fwd(3)
    w_own(near)
    ring(0, 1)
    ring(0, 2)
    gate_up(1)
    gate_up(2)
    ring(0, 3)
    gate_up(3)
    w_own(far)
    ring(1, 1)
    ring(2, 1)
    ring(3, 1)
    ring(0, 4)
    ring(1, 2)
    ring(2, 2)
    ring(3, 2)
    w_fwd(near)
    ring(1, 3)
    ring(2, 3)
    ring(3, 3)
    w_fwd(far)
    ready(0)
    project(0, 0)
    project(0, 1)
    ring(1, 4)
    ring(2, 4)
    ready(1)
    project(1, 0)
    project(1, 1)
    ring(3, 4)
    ready(2)
    project(2, 0)
    project(2, 1)
    ready(3)

    for g in range(2):
        project(3, g)
        for ty in range(NY):
            for k in range(8):
                first = (((k // 2) * NY + ty) * NC + k % 2) * OWN
                st[g, ty, pl.ds(k * PAD, PAD)] = acc[g, pl.ds(first, PAD)].astype(jnp.bfloat16)
        for d in range(1, NY):
            ty = lax.rem(y + d, NY)
            send(st.at[g, ty], rv.at[g, 3 - d], r_ss.at[g, d - 1], r_rs.at[g, 3 - d], dev(x, ty, z, c))

    cols = pl.ds(pl.multiple_of((z * NC + c) * dcols, 128), dcols)
    for g in range(2):
        total = st[g, y].astype(jnp.float32)
        for k in range(3):
            take(rv.at[g, k], r_rs.at[g, k])
            total += rv[g, k].astype(jnp.float32)
        fin[g] = total.astype(jnp.bfloat16)

        def place(k, _):
            tz, tc = 2 * (k // 2) + g, k % 2
            src = fin.at[g, pl.ds(pl.multiple_of(k * PAD, PAD), PAD)]
            here = jnp.logical_and(tz == z, tc == c)

            @pl.when(here)
            def _():
                pltpu.make_async_copy(src, fo.at[:, cols], f_rs).start()

            @pl.when(jnp.logical_not(here))
            def _():
                send(src, fo.at[:, cols], f_ss, f_rs, dev(x, y, tz, tc))

            return 0

        lax.fori_loop(0, 8, place, 0)
    take(fo, f_rs)
    for n in range(2 * NZ * NC):
        zh, yy, core = n // 8, (n // 2) % 4, n % 2
        at = (((2 * zh + core) * NC + yy // 2) * 2 + yy % 2) * piece
        out_ref[:, n * piece:(n + 1) * piece] = fo[:, at:at + piece]

    take(w_hbm.at[pl.ds(0, 2)], a_ss)
    for j in range(NY):
        src = w_hbm.at[2, :, pl.ds(0, 512)]
        if j == 0:
            @pl.when(jnp.logical_not(w_here))
            def _():
                take(src, w_ss.at[0])
        else:
            take(src, w_ss.at[j])
    for k in range(2):
        take(tok.at[0, pl.ds(0, quarter), pl.ds(0, 2 * chunk)], tk_ss.at[k])
        take(gu.at[0], xo_ss.at[k])
        take(gu.at[0, 0], xf_ss.at[k])
        take(wd.at[0], wo_ss.at[k])
        take(wd.at[0, pl.ds(0, piece)], wf_ss.at[k])
    for r in range(4):
        take(px.at[r], p_ss.at[r])
        take(hid.at[c, r], s_ss.at[r])
        for k in range(2):
            for d in range(4):
                h = hrows if d == 3 else rows
                take(hid.at[c, r, pl.ds(0, h), lane], h_ss.at[r, k, d])
    for k in range(2):
        take(tok.at[0, pl.ds(0, quarter)], ty_ss.at[k])
        take(tok.at[0, pl.ds(0, quarter), pl.ds(0, 2 * chunk)], ty_ss.at[2 + k])
    for k in range(3):
        for g in range(2):
            take(rv.at[g, k], r_ss.at[g, k])
    take(fin.at[0], f_ss)
    take(fin.at[1, pl.ds(0, 7 * PAD)], f_ss)


def per_device(tokens, routes, route_weights, ffn_weights):
    rows, width = tokens.shape
    w = ffn_weights.reshape(ffn_weights.shape[1], ffn_weights.shape[2], ffn_weights.shape[4])
    piece = w.shape[1]
    half = width // 2
    dcols = width // 16
    bf, f32 = jnp.bfloat16, jnp.float32
    dma = pltpu.SemaphoreType.DMA
    summed = pl.pallas_call(
        kernel,
        out_shape=jax.ShapeDtypeStruct((PAD, width), bf),
        in_specs=[pl.BlockSpec(memory_space=pl.ANY)] * 2,
        out_specs=pl.BlockSpec(memory_space=pltpu.VMEM),
        scratch_shapes=[
            pltpu.VMEM((2, rows, half), bf),
            pltpu.VMEM((4, 2, half, 128), bf),
            pltpu.VMEM((4, 2 * piece, 1024), bf),
            pltpu.VMEM((4, rows, 256), f32),
            pltpu.VMEM((4, rows, 256), f32),
            pltpu.VMEM((rows, 256), f32),
            pltpu.VMEM((2, 4, rows, 1024), bf),
            pltpu.VMEM((2, rows + 8, dcols), f32),
            pltpu.VMEM((2, NY, 8 * PAD, dcols), bf),
            pltpu.VMEM((2, 3, 8 * PAD, dcols), bf),
            pltpu.VMEM((2, 8 * PAD, dcols), bf),
            pltpu.VMEM((PAD, width), bf),
            dma,
            dma((2,)),
            dma((2,)),
            dma,
            dma((16,)),
            dma((2,)),
            dma((3, 16)),
            dma((2,)),
            dma((4,)),
            dma((4,)),
            dma((2,)),
            dma((3, 4)),
            dma((2,)),
            dma((4,)),
            dma((4,)),
            dma((4, 2, 4)),
            dma((4, 2, 5)),
            dma((4,)),
            dma((4,)),
            dma((2, 3)),
            dma((2, 3)),
            dma,
            dma,
            dma((4,)),
            dma((4,)),
        ],
        compiler_params=pltpu.CompilerParams(
            collective_id=0, has_side_effects=True, vmem_limit_bytes=56 * 2**20
        ),
    )(tokens, w)
    first = lax.axis_index("tp") * OWN
    matched = lax.dynamic_slice_in_dim(routes, first, OWN) == 0
    weights = lax.dynamic_slice_in_dim(route_weights, first, OWN)
    mix = jnp.sum(jnp.where(matched, weights, 0.0), axis=1)
    return (summed[:OWN].astype(f32) * mix[:, None]).astype(bf)


def solution(mesh):
    placed = (
        P("group", None),
        P("group", None),
        P("group", None),
        P(None, None, "tp", "group", None),
    )
    return jax.shard_map(
        per_device, mesh=mesh, in_specs=placed, out_specs=P(("group", "tp"), None), check_vma=False
    )
```

```python
import jax
import jax.numpy as jnp
from jax import lax
from jax.experimental import pallas as pl
from jax.experimental.pallas import tpu as pltpu
from jax.sharding import PartitionSpec as P

MESH = pl.DeviceIdType.MESH
NX, NY, NZ, NC = 4, 4, 8, 2
OWN = 14
PAD = 16


def dev(x, y, z, c):
    x, y, z = lax.rem(x + 2 * NX, NX), lax.rem(y + 2 * NY, NY), lax.rem(z + 2 * NZ, NZ)
    return ((z % 2) * NX + x, ((z // 2) * NY + y) * NC + c)


def take(ref, sem):
    pltpu.make_async_copy(ref, ref, sem).wait()


def kernel(tok_hbm, w_hbm, out_ref, tok, gu, wd, px, pr, po, hid, acc, st, rv, fin, fo,
           tok_sem, tk_ss, tk_rs, a_ss, a_rs, xo_ss, x_rs, xf_ss, w_ss, w_rs, wo_ss, wx_rs, wf_ss,
           p_ss, p_rs, h_ss, h_rs, s_ss, s_rs, r_ss, r_rs, f_ss, f_rs, ty_ss, ty_rs):
    grp, tp = lax.axis_index("group"), lax.axis_index("tp")
    z_lo, x = grp // NX, grp % NX
    c, y, z_hi = tp % NC, (tp // NC) % NY, tp // (NC * NY)
    z = z_hi * 2 + z_lo
    rows = tok.shape[1]
    half = tok.shape[2]
    piece = w_hbm.shape[1]
    hrows = rows // 2
    dcols = acc.shape[2]

    def send(src, dst, ss, rs, to):
        pltpu.make_async_remote_copy(
            src_ref=src, dst_ref=dst, send_sem=ss, recv_sem=rs, device_id=to, device_id_type=MESH
        ).start()

    right, left = dev(x + 1, y, z, c), dev(x - 1, y, z, c)
    up, down = dev(x, y, z + 1, c), dev(x, y, z - 1, c)
    north, south = dev(x, y + 1, z, c), dev(x, y - 1, z, c)
    sib = dev(x, y, z, 1 - c)
    chunk = half // 4

    def at_hbm(k):
        return pl.ds(pl.multiple_of((2 * k + c) * chunk, 128), chunk)

    for k in range(4):
        pltpu.make_async_copy(
            tok_hbm.at[:, at_hbm(k)], tok.at[z_lo, :, pl.ds(k * chunk, chunk)], tok_sem
        ).start()

    bar = pltpu.get_barrier_semaphore()
    me = (z * NY + y) * NC + c
    plane = NZ * NY * NC

    def hello(i, _):
        j = lax.rem(me + i, plane)
        to = dev(x, (j // NC) % NY, j // (NC * NY), j % NC)
        pl.semaphore_signal(bar, inc=1, device_id=to, device_id_type=MESH)
        return 0

    lax.fori_loop(1, plane, hello, 0)
    pl.semaphore_signal(bar, inc=1, device_id=right, device_id_type=MESH)
    pl.semaphore_signal(bar, inc=1, device_id=left, device_id_type=MESH)
    pl.semaphore_wait(bar, plane + 1)

    src_slot = z_hi * 4 + (y % 2) * NC + c
    src_rows = pl.ds(pl.multiple_of(src_slot * piece, 64), piece)

    def a_wave(w):
        far = 1 + 2 * (w // 2)
        for dy in (w % 2, w % 2 + 2):
            for dz in (far, -far):
                ty, tz = lax.rem(y + dy, NY), lax.rem(z + dz + NZ, NZ)
                lanes = pl.ds(pl.multiple_of((ty * 4 + tz // 2) * 128, 128), 128)
                send(w_hbm.at[pl.ds(0, 2), :, lanes], gu.at[0, :, src_rows, :], a_ss,
                     a_rs.at[src_slot], dev(x, ty, tz, y // 2))

    wz, wc = 2 * z_hi + c, y // 2
    w_here = jnp.logical_and(wz == z, wc == c)
    w_dst = wd.at[0, pl.ds(pl.multiple_of((y % 2) * piece, 64), piece),
                  pl.ds(pl.multiple_of(z_lo * 512, 128), 512)]

    def w_send():
        for j in range(NY):
            ty = lax.rem(y + j, NY)
            src = w_hbm.at[2, :, pl.ds(pl.multiple_of(ty * 512, 128), 512)]
            rs = w_rs.at[z_lo * 2 + y % 2]
            if j == 0:
                @pl.when(w_here)
                def _():
                    pltpu.make_async_copy(src, w_dst, rs).start()

                @pl.when(jnp.logical_not(w_here))
                def _():
                    send(src, w_dst, w_ss.at[0], rs, dev(x, ty, wz, wc))
            else:
                send(src, w_dst, w_ss.at[j], rs, dev(x, ty, wz, wc))

    quarter = rows // NY

    def quarter_of(yy):
        return pl.ds(pl.multiple_of(yy * quarter, PAD), quarter)

    def tok_send():
        for k in range(4):
            send(tok_hbm.at[quarter_of(y), at_hbm(k)],
                 tok.at[z_lo, quarter_of(y), pl.ds(k * chunk, chunk)],
                 tk_ss.at[k // 2], tk_rs.at[k // 2], down if k // 2 else up)

    def tok_pass():
        for k in range(2):
            take(tok.at[1 - z_lo, quarter_of(y), pl.ds(2 * k * chunk, 2 * chunk)], tk_rs.at[k])
        mine = tok.at[1 - z_lo, quarter_of(y)]
        send(mine, mine, ty_ss.at[0], ty_rs.at[0], north)
        send(mine, mine, ty_ss.at[1], ty_rs.at[1], south)

    def tok_fwd():
        for k, to in ((0, north), (1, south)):
            yy = quarter_of(lax.rem(y + (1 if k else NY - 1), NY))
            take(tok.at[1 - z_lo, yy], ty_rs.at[k])
            part = tok.at[1 - z_lo, yy, pl.ds(2 * k * chunk, 2 * chunk)]
            send(part, part, ty_ss.at[2 + k], ty_rs.at[2 + k], to)

    def tok_wait():
        take(tok.at[z_lo], tok_sem)
        for k in range(2):
            yy = quarter_of(lax.rem(y + 2, NY))
            take(tok.at[1 - z_lo, yy, pl.ds(2 * k * chunk, 2 * chunk)], ty_rs.at[2 + k])

    def slot_of(w, m):
        far = (1 + 2 * (w // 2)) * (1 - 2 * m)
        return (lax.rem(z - far + NZ, NZ) // 2) * 4 + ((y + w) % 2) * NC

    def pc(k, s):
        return gu.at[k, :, pl.ds(pl.multiple_of(s * piece, 64), piece), :]

    def x_own(w):
        for m in range(2):
            for core in range(NC):
                s = slot_of(w, m) + core
                take(pc(0, s), a_rs.at[s])
                send(pc(0, s), pc(1, s), xo_ss.at[0], x_rs.at[0, s], right)
                send(pc(0, s), pc(2, s), xo_ss.at[1], x_rs.at[1, s], left)

    def x_fwd(w):
        for m in range(2):
            s = slot_of(w, m)
            take(pc(1, s), x_rs.at[0, s])
            send(pc(1, s), pc(3, s), xf_ss.at[0], x_rs.at[2, s], right)
            take(pc(2, s + 1), x_rs.at[1, s + 1])
            send(pc(2, s + 1), pc(3, s + 1), xf_ss.at[1], x_rs.at[2, s + 1], left)

    def wpc(k, i):
        return wd.at[k, pl.ds(pl.multiple_of((i % 2) * piece, 64), piece),
                     pl.ds(pl.multiple_of((i // 2) * 512, 128), 512)]

    near = z_lo * 2
    far = 2 - near

    def w_own(first):
        for i in (first, first + 1):
            take(wpc(0, i), w_rs.at[i])
            send(wpc(0, i), wpc(1, i), wo_ss.at[0], wx_rs.at[0, i], right)
            send(wpc(0, i), wpc(2, i), wo_ss.at[1], wx_rs.at[1, i], left)

    def w_fwd(i):
        take(wpc(1, i), wx_rs.at[0, i])
        send(wpc(1, i), wpc(3, i), wf_ss.at[0], wx_rs.at[2, i], right)
        take(wpc(2, i + 1), wx_rs.at[1, i + 1])
        send(wpc(2, i + 1), wpc(3, i + 1), wf_ss.at[1], wx_rs.at[2, i + 1], left)

    lane = pl.ds(pl.multiple_of(((1 - z_lo) * 4 + z_hi) * 128, 128), 128)

    def gate_up(r):
        if r == 1:
            for n in range(8):
                take(pc(1, 2 * n + 1), x_rs.at[0, 2 * n + 1])
        if r == 2:
            for n in range(8):
                take(pc(2, 2 * n), x_rs.at[1, 2 * n])
        if r == 3:
            for n in range(16):
                take(pc(3, n), x_rs.at[2, n])
        rhs = jnp.concatenate([gu[r, 0], gu[r, 1]], axis=1)
        px[r] = jnp.dot(tok[1 - c], rhs, preferred_element_type=jnp.float32)
        send(px.at[r], pr.at[r], p_ss.at[r], p_rs.at[r], sib)
        po[...] = jnp.dot(tok[c], rhs, preferred_element_type=jnp.float32)
        take(pr.at[r], p_rs.at[r])
        gate = po[:, :128] + pr[r, :, :128]
        upv = po[:, 128:] + pr[r, :, 128:]
        hid[c, r, :, lane] = (gate / (1.0 + jnp.exp(-gate)) * upv).astype(jnp.bfloat16)
        own = hid.at[c, r, :, lane]
        send(own, own, h_ss.at[r, 0, 0], h_rs.at[r, 0, 1], up)
        send(own, own, h_ss.at[r, 1, 0], h_rs.at[r, 1, 1], down)
        send(own, own, s_ss.at[r], s_rs.at[r], sib)

    def ring(r, d):
        for k, to in ((0, up), (1, down)):
            zs = lax.rem(z + (d if k else NZ - d), NZ)
            ln = pl.ds(pl.multiple_of(((1 - zs % 2) * 4 + zs // 2) * 128, 128), 128)
            part = pl.ds(k * hrows, hrows)
            got = hid.at[c, r, part, ln] if d == 4 else hid.at[c, r, :, ln]
            take(got, h_rs.at[r, k, d])
            if d < 3:
                send(got, got, h_ss.at[r, k, d], h_rs.at[r, k, d + 1], to)
            elif d == 3:
                more = hid.at[c, r, part, ln]
                send(more, more, h_ss.at[r, k, d], h_rs.at[r, k, d + 1], to)
            send(got, got, s_ss.at[r], s_rs.at[r], sib)

    def ready(r):
        take(hid.at[1 - c, r], s_rs.at[r])
        if r == 1:
            for i in (1, 3):
                take(wpc(1, i), wx_rs.at[0, i])
        if r == 2:
            for i in (0, 2):
                take(wpc(2, i), wx_rs.at[1, i])
        if r == 3:
            for i in range(4):
                take(wpc(3, i), wx_rs.at[2, i])

    def project(r, g):
        term = lax.dot_general(hid[g, r], wd[r], (((1,), (1,)), ((), ())),
                               preferred_element_type=jnp.float32)
        if r == 0:
            acc[g, pl.ds(0, rows)] = term
        else:
            acc[g, pl.ds(0, rows)] += term

    acc[:, pl.ds(rows, 8)] = jnp.zeros((2, 8, dcols), jnp.float32)
    a_wave(0)
    pl.when(c == z_lo)(w_send)
    x_own(0)
    tok_send()
    a_wave(1)
    tok_pass()
    a_wave(2)
    x_fwd(0)
    x_own(1)
    x_fwd(1)
    a_wave(3)
    tok_fwd()
    x_own(2)
    pl.when(c != z_lo)(w_send)
    x_fwd(2)
    x_own(3)
    tok_wait()
    gate_up(0)
    x_fwd(3)
    w_own(near)
    ring(0, 1)
    gate_up(1)
    ring(0, 2)
    gate_up(2)
    ring(0, 3)
    ring(1, 1)
    gate_up(3)
    w_own(far)
    ring(2, 1)
    ring(3, 1)
    ring(0, 4)
    ring(1, 2)
    ring(2, 2)
    ring(3, 2)
    w_fwd(near)
    ring(1, 3)
    ring(2, 3)
    ring(3, 3)
    w_fwd(far)
    ready(0)
    project(0, 0)
    project(0, 1)
    ring(1, 4)
    ring(2, 4)
    ready(1)
    project(1, 0)
    project(1, 1)
    ring(3, 4)
    ready(2)
    project(2, 0)
    project(2, 1)
    ready(3)

    for g in range(2):
        project(3, g)
        for ty in range(NY):
            for k in range(8):
                first = (((k // 2) * NY + ty) * NC + k % 2) * OWN
                st[g, ty, pl.ds(k * PAD, PAD)] = acc[g, pl.ds(first, PAD)].astype(jnp.bfloat16)
        for d in range(1, NY):
            ty = lax.rem(y + d, NY)
            send(st.at[g, ty], rv.at[g, 3 - d], r_ss.at[g, d - 1], r_rs.at[g, 3 - d], dev(x, ty, z, c))

    cols = pl.ds(pl.multiple_of((z * NC + c) * dcols, 128), dcols)
    for g in range(2):
        total = st[g, y].astype(jnp.float32)
        for k in range(3):
            take(rv.at[g, k], r_rs.at[g, k])
            total += rv[g, k].astype(jnp.float32)
        fin[g] = total.astype(jnp.bfloat16)

        def place(k, _):
            tz, tc = 2 * (k // 2) + g, k % 2
            src = fin.at[g, pl.ds(pl.multiple_of(k * PAD, PAD), PAD)]
            here = jnp.logical_and(tz == z, tc == c)

            @pl.when(here)
            def _():
                pltpu.make_async_copy(src, fo.at[:, cols], f_rs).start()

            @pl.when(jnp.logical_not(here))
            def _():
                send(src, fo.at[:, cols], f_ss, f_rs, dev(x, y, tz, tc))

            return 0

        lax.fori_loop(0, 8, place, 0)
    take(fo, f_rs)
    for n in range(2 * NZ * NC):
        zh, yy, core = n // 8, (n // 2) % 4, n % 2
        at = (((2 * zh + core) * NC + yy // 2) * 2 + yy % 2) * piece
        out_ref[:, n * piece:(n + 1) * piece] = fo[:, at:at + piece]

    take(w_hbm.at[pl.ds(0, 2)], a_ss)
    for j in range(NY):
        src = w_hbm.at[2, :, pl.ds(0, 512)]
        if j == 0:
            @pl.when(jnp.logical_not(w_here))
            def _():
                take(src, w_ss.at[0])
        else:
            take(src, w_ss.at[j])
    for k in range(2):
        take(tok.at[0, pl.ds(0, quarter), pl.ds(0, 2 * chunk)], tk_ss.at[k])
        take(gu.at[0], xo_ss.at[k])
        take(gu.at[0, 0], xf_ss.at[k])
        take(wd.at[0], wo_ss.at[k])
        take(wd.at[0, pl.ds(0, piece)], wf_ss.at[k])
    for r in range(4):
        take(px.at[r], p_ss.at[r])
        take(hid.at[c, r], s_ss.at[r])
        for k in range(2):
            for d in range(4):
                h = hrows if d == 3 else rows
                take(hid.at[c, r, pl.ds(0, h), lane], h_ss.at[r, k, d])
    for k in range(2):
        take(tok.at[0, pl.ds(0, quarter)], ty_ss.at[k])
        take(tok.at[0, pl.ds(0, quarter), pl.ds(0, 2 * chunk)], ty_ss.at[2 + k])
    for k in range(3):
        for g in range(2):
            take(rv.at[g, k], r_ss.at[g, k])
    take(fin.at[0], f_ss)
    take(fin.at[1, pl.ds(0, 7 * PAD)], f_ss)


def per_device(tokens, routes, route_weights, ffn_weights):
    rows, width = tokens.shape
    w = ffn_weights.reshape(ffn_weights.shape[1], ffn_weights.shape[2], ffn_weights.shape[4])
    piece = w.shape[1]
    half = width // 2
    dcols = width // 16
    bf, f32 = jnp.bfloat16, jnp.float32
    dma = pltpu.SemaphoreType.DMA
    summed = pl.pallas_call(
        kernel,
        out_shape=jax.ShapeDtypeStruct((PAD, width), bf),
        in_specs=[pl.BlockSpec(memory_space=pl.ANY)] * 2,
        out_specs=pl.BlockSpec(memory_space=pltpu.VMEM),
        scratch_shapes=[
            pltpu.VMEM((2, rows, half), bf),
            pltpu.VMEM((4, 2, half, 128), bf),
            pltpu.VMEM((4, 2 * piece, 1024), bf),
            pltpu.VMEM((4, rows, 256), f32),
            pltpu.VMEM((4, rows, 256), f32),
            pltpu.VMEM((rows, 256), f32),
            pltpu.VMEM((2, 4, rows, 1024), bf),
            pltpu.VMEM((2, rows + 8, dcols), f32),
            pltpu.VMEM((2, NY, 8 * PAD, dcols), bf),
            pltpu.VMEM((2, 3, 8 * PAD, dcols), bf),
            pltpu.VMEM((2, 8 * PAD, dcols), bf),
            pltpu.VMEM((PAD, width), bf),
            dma,
            dma((2,)),
            dma((2,)),
            dma,
            dma((16,)),
            dma((2,)),
            dma((3, 16)),
            dma((2,)),
            dma((4,)),
            dma((4,)),
            dma((2,)),
            dma((3, 4)),
            dma((2,)),
            dma((4,)),
            dma((4,)),
            dma((4, 2, 4)),
            dma((4, 2, 5)),
            dma((4,)),
            dma((4,)),
            dma((2, 3)),
            dma((2, 3)),
            dma,
            dma,
            dma((4,)),
            dma((4,)),
        ],
        compiler_params=pltpu.CompilerParams(
            collective_id=0, has_side_effects=True, vmem_limit_bytes=56 * 2**20
        ),
    )(tokens, w)
    first = lax.axis_index("tp") * OWN
    matched = lax.dynamic_slice_in_dim(routes, first, OWN) == 0
    weights = lax.dynamic_slice_in_dim(route_weights, first, OWN)
    mix = jnp.sum(jnp.where(matched, weights, 0.0), axis=1)
    return (summed[:OWN].astype(f32) * mix[:, None]).astype(bf)


def solution(mesh):
    placed = (
        P("group", None),
        P("group", None),
        P("group", None),
        P(None, None, "tp", "group", None),
    )
    return jax.shard_map(
        per_device, mesh=mesh, in_specs=placed, out_specs=P(("group", "tp"), None), check_vma=False
    )
```
